128 devices in a mesh: dom: 16 (over x, z), sub: 8 (over y, core).
Axes of the slice: x: 4, y: 4, z: 4, core: 2. Of those that a mesh axis runs over, the one named last changes fastest.
Arguments:
- segments: float32 [16384, 9, 128], P(('dom', 'sub')), may hold values from -6 to 6
- send_tiles: int32 [128, 128, 4], P(('dom', 'sub')), may hold values from 0 to 127
- pair_local: int32 [128, 512], P(('dom', 'sub')), may hold values from 0 to 127
- pair_remote: int32 [128, 512], P(('dom', 'sub')), may hold values from 0 to 511, each once within a row
- pair_count: int32 [128], P(('dom', 'sub')), may hold values from 64 to 512, as said below
- tile_cell: int32 [16384], P(('dom', 'sub')), may hold values from 0 to 63
Outputs:
- forces: float32 [16384, 3, 128], P(('dom', 'sub'))
The draws below stay inside these ranges and needn't reach their ends.
Inputs may be any that keep to these rules, and one draw needn't show every extreme that they name: `send_tiles`: every slot names a tile; each device sends exactly 4 tiles to every device. `pair_remote`: each device's row names every one of its 512 received slots once. `pair_count`: some device holds 512 live pairs.
All inputs are finite; a program needn't handle non-finite values.
Results may differ from the reference program's by a relative error of at most 0.00018.
Values sent between devices are 32-bit elements; how exact they have to be, the bound alone decides.
A program may use at most 64 MiB of HBM per device.

```python
import jax
import jax.numpy as jnp
from jax import lax

TILE = 128
TILES_DEV = 128
PAIRS_DEV = 512
BLOCK = 64
NCELL = 64
CAP = 4
TILES = 16384
DEVICES = 128


def draw_pair_count(key, part):
    key = jax.random.fold_in(key, 7)
    first, second = jax.random.split(key)
    lighter = jax.random.randint(first, (DEVICES,), PAIRS_DEV // 8, PAIRS_DEV // 2 + 1)
    busiest = jax.random.randint(second, (), 0, DEVICES)
    return jnp.where(jnp.arange(DEVICES) == busiest, PAIRS_DEV, lighter).astype(jnp.int32)


def touch_ends(array, stream_key, low, high):
    shape = array.shape
    place = [jax.random.randint(jax.random.fold_in(stream_key, axis), (), 0, shape[axis]) for axis in range(len(shape))]
    array = array.at[tuple(place)].set(low)
    longest = shape.index(max(shape))
    place[longest] = (place[longest] + 1) % shape[longest]
    return array.at[tuple(place)].set(high)


def block_scale(stream_key, extent, cuts, low, largest):
    gain, own = 1.0, jax.random.fold_in(stream_key, 6)
    for axis_at, parts in cuts:
        draws = jnp.exp(jax.random.uniform(jax.random.fold_in(own, axis_at), (parts,), jnp.float32, low / len(cuts), largest / len(cuts)))
        gain = gain * jnp.repeat(draws, extent[axis_at] // parts).reshape([-1 if axis == axis_at else 1 for axis in range(len(extent))])
    return gain


def bell_draw(stream_key, extent, scale, reach, pieces=(), dtype=jnp.bfloat16):
    array = jax.random.normal(stream_key, extent, jnp.float32) * scale
    if len(pieces) > 0:
        array = block_scale(stream_key, extent, pieces, -0.22, 0.18) * array
    return jnp.clip(array, min=-reach, max=reach).astype(dtype)


def setup_inputs(seed: int = 0) -> dict:
    arg_keys = jax.random.split(jax.random.key(seed), 7)
    return {
        "segments": bell_draw(arg_keys[0], (TILES, 9, TILE), 1.0, 6.0, ((0, 128),), jnp.float32),
        "send_tiles": touch_ends(jax.random.randint(arg_keys[1], (DEVICES, DEVICES, CAP), 0, TILES_DEV), jax.random.fold_in(arg_keys[1], 1), 0, TILES_DEV - 1).astype(jnp.int32),
        "pair_local": touch_ends(jax.random.randint(arg_keys[2], (DEVICES, PAIRS_DEV), 0, TILES_DEV), jax.random.fold_in(arg_keys[2], 1), 0, TILES_DEV - 1).astype(jnp.int32),
        "pair_remote": jax.vmap(lambda own: jax.random.permutation(own, PAIRS_DEV))(jax.random.split(arg_keys[3], DEVICES)).reshape((DEVICES, PAIRS_DEV)).astype(jnp.int32),
        "pair_count": draw_pair_count(jax.random.fold_in(arg_keys[6], 71), 0),
        "tile_cell": touch_ends(jax.random.randint(arg_keys[5], (TILES,), 0, NCELL), jax.random.fold_in(arg_keys[5], 1), 0, NCELL - 1).astype(jnp.int32),
    }


core_square = 0.25

def interact(near_block, far_block, live_mask):
    apart = near_block[:, 0:3, :, None] - far_block[:, 0:3, None, :]
    spread = lax.optimization_barrier(jnp.sum(apart * apart, axis=1)) + core_square
    inverse = lax.rsqrt(spread)
    inverse = inverse * inverse * inverse
    burgers_dot = lax.optimization_barrier(jnp.sum(near_block[:, 3:6, :, None] * far_block[:, 3:6, None, :], axis=1))
    cross_first = lax.optimization_barrier(jnp.sum(near_block[:, 3:6, :, None] * far_block[:, 6:9, None, :], axis=1))
    cross_second = lax.optimization_barrier(jnp.sum(far_block[:, 3:6, None, :] * near_block[:, 6:9, :, None], axis=1))
    coupling = (burgers_dot + cross_first * cross_second) * inverse * live_mask[:, None, None]
    weighted = apart * coupling[:, None]
    return (lax.optimization_barrier(jnp.sum(weighted, axis=3)), -lax.optimization_barrier(jnp.sum(weighted, axis=2)))

def far_field(segments, tile_cell, moment_sums, total_segments):
    moments = moment_sums.reshape(NCELL, 3, 3) / jnp.sqrt(jnp.float32(total_segments))
    moments = 0.5 * (moments + jnp.transpose(moments, (0, 2, 1)))
    cells = jnp.arange(NCELL).astype(jnp.float32)
    weights = 8.0 / (8.0 + jnp.abs(cells[:, None] - cells[None, :]))
    stress = jnp.dot(weights, moments.reshape(NCELL, 9), precision=lax.Precision.HIGHEST)
    onehot = (tile_cell[:, None] == jnp.arange(NCELL)[None, :]).astype(jnp.float32)
    tile_stress = jnp.dot(onehot, stress, precision=lax.Precision.HIGHEST).reshape(-1, 3, 3)
    traction = lax.optimization_barrier(jnp.sum(tile_stress[:, :, :, None] * segments[:, None, 3:6, :], axis=2))
    lines = segments[:, 6:9, :]
    return jnp.stack([traction[:, 1] * lines[:, 2] - traction[:, 2] * lines[:, 1], traction[:, 2] * lines[:, 0] - traction[:, 0] * lines[:, 2], traction[:, 0] * lines[:, 1] - traction[:, 1] * lines[:, 0]], axis=1)

def local_moments(segments, tile_cell):
    outer = lax.optimization_barrier(jnp.sum(segments[:, 3:6, None, :] * segments[:, None, 6:9, :], axis=3)).reshape(-1, 9)
    onehot = (jnp.arange(NCELL)[:, None] == tile_cell[None, :]).astype(jnp.float32)
    return jnp.dot(onehot, outer, precision=lax.Precision.HIGHEST)

def reference(segments, send_tiles, pair_local, pair_remote, pair_count, tile_cell):
    devices = send_tiles.shape[0]
    slots = send_tiles.shape[2]
    tiles_dev = segments.shape[0] // devices
    owner = jnp.arange(devices).astype(jnp.int32)[:, None]
    source = pair_remote // slots
    column = pair_remote % slots
    far_tile = (source * tiles_dev + send_tiles[source, owner, column]).astype(jnp.int32)
    near_tile = (owner * tiles_dev + pair_local).astype(jnp.int32)
    live = (jnp.arange(PAIRS_DEV)[None, :] < pair_count[:, None]).astype(jnp.float32)
    near_blocks = near_tile.reshape(-1, BLOCK)
    far_blocks = far_tile.reshape(-1, BLOCK)
    live_blocks = live.reshape(-1, BLOCK)

    def advance(totals, inputs):
        near_ids, far_ids, live_mask = inputs
        near_part, far_part = interact(segments[near_ids], segments[far_ids], live_mask)
        totals = totals.at[near_ids].add(near_part)
        totals = totals.at[far_ids].add(far_part)
        return (totals, None)
    start = jnp.zeros((segments.shape[0], 3, segments.shape[2]), jnp.float32)
    pair_forces, unused = lax.scan(advance, start, (near_blocks, far_blocks, live_blocks))
    moment_sums = local_moments(segments, tile_cell)
    total_segments = segments.shape[0] * segments.shape[2]
    return pair_forces + far_field(segments, tile_cell, moment_sums, total_segments)
```

```python
import functools

import jax
import jax.numpy as jnp
from jax import lax
from jax.experimental import pallas as pl
from jax.experimental.pallas import tpu as pltpu
from jax.sharding import PartitionSpec as P

NCELL = 64
CAP = 4
PEERS = 128
MESH = pl.DeviceIdType.MESH
f32 = jnp.float32
bf16 = jnp.bfloat16

GROUP = 4
KNUM = 48
KDIST = 32
K = KNUM + KDIST
FROWS = K + 16
NT = (((1,), (1,)), ((), ()))


def top(v):
    return v.astype(bf16).astype(f32)


def split2(v):
    h = top(v)
    return h, v - h


def split3(v):
    h = top(v)
    r = v - h
    m = top(r)
    return h, m, r - m


def near_rows(x, b, l):
    vals = list(b) + [b[i] * l[j] for i in range(3) for j in range(3)]
    hl = [split2(v) for v in vals]
    zero = jnp.zeros_like(x[0])
    one = zero + 1.0
    num = [h for h, _ in hl] + [h for h, _ in hl] + [lo for _, lo in hl]
    num += [zero] * (KNUM - 36)
    xs = [split3(v) for v in x]
    hi, mid, low = [[s[i] for s in xs] for i in range(3)]
    q = split3(x[0] * x[0] + x[1] * x[1] + x[2] * x[2] + 0.25)
    dist = hi + hi + mid + hi + low + mid + list(q) + [one] * 3
    dist += [zero] * (KDIST - 24)
    return num + dist + list(x)


def far_rows(x, b, l):
    vals = list(b) + [l[i] * b[j] for i in range(3) for j in range(3)]
    hl = [split2(v) for v in vals]
    zero = jnp.zeros_like(x[0])
    one = zero + 1.0
    num = [h for h, _ in hl] + [lo for _, lo in hl] + [h for h, _ in hl]
    num += [zero] * (KNUM - 36)
    xs = [split3(v) for v in x]
    hi, mid, low = [[s[i] for s in xs] for i in range(3)]
    q = split3(x[0] * x[0] + x[1] * x[1] + x[2] * x[2])
    neg = lambda rows: [-2.0 * v for v in rows]
    nh, nm, nl = neg(hi), neg(mid), neg(low)
    dist = nh + nm + nh + nl + nh + nm + [one] * 3 + list(q)
    dist += [zero] * (KDIST - 24)
    two = [v - h for v, h in zip(x, hi)]
    sums = hi + [one] + [zero] * 4 + two + [zero] * 5
    return num + dist + sums


def put(scr, rows, count):
    for f, v in enumerate(rows):
        scr[8 * f : 8 * f + count, :] = v


def prepare_near(seg, nft, spread, scr):
    def body(g, carry):
        tiles = pl.ds(pl.multiple_of(g * 8, 8), 8)
        comp = [seg[tiles, a, :] for a in range(9)]
        rows = near_rows(comp[0:3], comp[3:6], comp[6:9])
        put(scr, rows, 8)
        for c in range(8):
            feat = scr[pl.ds(c, K + 8, stride=8), :]
            feat = jnp.concatenate([feat, jnp.zeros((128 - K - 8, 128), f32)], 0).T
            nft[g * 8 + c] = feat.astype(bf16)
            for a in range(3):
                spread[g * 8 + c, 128 * a : 128 * a + 128, :] = jnp.broadcast_to(
                    feat[:, K + a : K + a + 1], (128, 128)
                )
        return carry

    lax.fori_loop(0, 16, body, 0)


def block(comp, live, nears, nft, spread, scr, part):
    x, b, l = comp[0:3], [v * live for v in comp[3:6]], comp[6:9]
    put(scr, far_rows(x, b, l), CAP)
    near_parts = []
    zn = jnp.zeros((KNUM, 128), bf16)
    zd = jnp.zeros((KDIST, 128), bf16)
    for c in range(CAP):
        feat = scr[pl.ds(c, K, stride=8), :].astype(bf16)
        xf = scr[pl.ds(8 * K + c, 16, stride=8), :].astype(bf16)
        right = jnp.concatenate(
            [
                jnp.concatenate([feat[:KNUM], zn], 1),
                jnp.concatenate([zd, feat[KNUM:]], 1),
            ],
            0,
        )
        n = nears[c]
        both = jnp.dot(nft[n][:, :K], right, preferred_element_type=f32)
        inv = lax.rsqrt(both[:, 128:])
        coup = both[:, :128] * (inv * inv * inv)
        hi = coup.astype(bf16)
        lo = (coup - hi.astype(f32)).astype(bf16)
        sn = lax.dot_general(
            jnp.concatenate([xf, xf], 1),
            jnp.concatenate([hi, lo], 1),
            NT,
            preferred_element_type=f32,
        )
        near_parts.append(sn[0:8] + sn[8:16])
        acc = [None] * 4
        for i in range(16):
            cv = coup[8 * i : 8 * i + 8]
            for a in range(3):
                t = cv * spread[n, 128 * a + 8 * i : 128 * a + 8 * i + 8, :]
                acc[a] = t if acc[a] is None else acc[a] + t
            acc[3] = cv if acc[3] is None else acc[3] + cv
        for a in range(4):
            part[32 * a + 8 * c : 32 * a + 8 * c + 8, :] = acc[a]
    sums = []
    for a in range(4):
        s = part[pl.ds(32 * a, CAP, stride=8), :]
        for i in range(1, 8):
            s = s + part[pl.ds(32 * a + i, CAP, stride=8), :]
        sums.append(s)
    far = [x[a] * sums[3] - sums[a] for a in range(3)]
    return far, near_parts


def offset(j):
    k = lax.rem(j * 37, PEERS)
    return lax.rem(lax.div(k, 32), 4), lax.rem(lax.div(k, 8), 4), lax.rem(lax.div(k, 2), 4), lax.rem(k, 2)


def shifted(d, s, j, sign):
    dx, dz, dy, dc = offset(j)
    if sign < 0:
        dx, dz, dy = 4 - dx, 4 - dz, 4 - dy
    x = lax.rem(lax.div(d, 4) + dx, 4)
    z = lax.rem(lax.rem(d, 4) + dz, 4)
    y = lax.rem(lax.div(s, 2) + dy, 4)
    c = lax.rem(lax.rem(s, 2) + dc, 2)
    return x * 4 + z, y * 2 + c


def exchange(
    near_ref, live_ref, send_ref, seg_hbm, mom_ref,
    nraw_ref, back_ref, total_ref,
    seg, stage, recv, back, nft, spread, nscr, scr, part, mom_a, mom_b,
    seg_sem, out_send, out_recv, back_send, back_recv, mom_sem, stage_sem,
):
    d = lax.axis_index("dom")
    s = lax.axis_index("sub")
    barrier = pltpu.get_barrier_semaphore()
    for k in range(1, 8):
        pl.semaphore_signal(barrier, inc=1, device_id=(d, lax.rem(s + k, 8)), device_id_type=MESH)
    for k in range(1, 16):
        pl.semaphore_signal(barrier, inc=1, device_id=(lax.rem(d + k, 16), s), device_id_type=MESH)
    load = pltpu.make_async_copy(seg_hbm, seg, seg_sem)
    load.start()
    load.wait()

    def gather(j, carry):
        td, ts = shifted(d, s, j, 1)
        base = (td * 8 + ts) * CAP
        for c in range(CAP):
            stage[j, 9 * c : 9 * c + 9, :] = seg[send_ref[base + c]]
        return carry

    lax.fori_loop(0, PEERS, gather, 0)
    recv[0] = stage[0]
    mom_a[0] = mom_ref[...]

    pl.semaphore_wait(barrier, 22)
    for k in range(1, 8):
        pl.semaphore_signal(stage_sem, inc=1, device_id=(d, lax.rem(s + k, 8)), device_id_type=MESH)
    pl.semaphore_wait(stage_sem, 7)

    def mom_copy_a(k):
        return pltpu.make_async_remote_copy(
            src_ref=mom_ref, dst_ref=mom_a.at[k], send_sem=mom_sem.at[0], recv_sem=mom_sem.at[1],
            device_id=(d, lax.rem(s + k, 8)), device_id_type=MESH)

    def mom_copy_b(k):
        return pltpu.make_async_remote_copy(
            src_ref=mom_b.at[0], dst_ref=mom_b.at[k], send_sem=mom_sem.at[2], recv_sem=mom_sem.at[3],
            device_id=(lax.rem(d + k, 16), s), device_id_type=MESH)

    for k in range(1, 8):
        mom_copy_a(k).start()

    def send(j, carry):
        pltpu.make_async_remote_copy(
            src_ref=stage.at[j], dst_ref=recv.at[j], send_sem=out_send, recv_sem=out_recv.at[lax.div(j, GROUP)],
            device_id=shifted(d, s, j, 1), device_id_type=MESH).start()
        return carry

    lax.fori_loop(1, PEERS, send, 0)
    prepare_near(seg, nft, spread, nscr)

    a_all = pltpu.make_async_remote_copy(
        src_ref=mom_a.at[pl.ds(1, 7)], dst_ref=mom_a.at[pl.ds(1, 7)], send_sem=mom_sem.at[0], recv_sem=mom_sem.at[1],
        device_id=(d, lax.rem(s + 1, 8)), device_id_type=MESH)
    a_all.wait_recv()
    mom_b[0] = jnp.sum(mom_a[...], 0)
    for k in range(1, 16):
        mom_copy_b(k).start()

    def wait_blocks(first, count, g):
        pltpu.make_async_remote_copy(
            src_ref=stage.at[pl.ds(first, count)], dst_ref=recv.at[pl.ds(first, count)],
            send_sem=out_send, recv_sem=out_recv.at[g],
            device_id=shifted(d, s, 1, 1), device_id_type=MESH).wait_recv()

    def back_copy(j):
        return pltpu.make_async_remote_copy(
            src_ref=stage.at[j, pl.ds(0, 12)], dst_ref=back.at[j], send_sem=back_send, recv_sem=back_recv,
            device_id=shifted(d, s, j, -1), device_id_type=MESH)

    rows = lax.broadcasted_iota(jnp.int32, (CAP, 128), 0)

    def work(g, carry):
        @pl.when(g == 0)
        def _():
            wait_blocks(1, GROUP - 1, 0)

        @pl.when(g > 0)
        def _():
            wait_blocks(g * GROUP, GROUP, g)

        for u in range(GROUP):
            j = g * GROUP + u
            td, ts = shifted(d, s, j, -1)
            base = (td * 8 + ts) * CAP
            comp = [recv[j, pl.ds(a, CAP, stride=9), :] for a in range(9)]
            live = jnp.full((CAP, 128), live_ref[base], f32)
            for c in range(1, CAP):
                live = jnp.where(rows == c, live_ref[base + c], live)
            nears = [near_ref[base + c] for c in range(CAP)]
            far, near = block(comp, live, nears, nft, spread, scr.at[u], part.at[u])
            for a in range(3):
                recv[j, CAP * a : CAP * a + CAP, :] = far[a]
            for c in range(CAP):
                nraw_ref[j, 4 * c : 4 * c + 4, :] = near[c][0:4]

        for u in range(GROUP):
            j = g * GROUP + u

            @pl.when(j > 0)
            def _():
                pltpu.make_async_remote_copy(
                    src_ref=recv.at[j, pl.ds(0, 12)], dst_ref=back.at[j], send_sem=back_send, recv_sem=back_recv,
                    device_id=shifted(d, s, j, -1), device_id_type=MESH).start()

        return carry

    lax.fori_loop(0, PEERS // GROUP, work, 0)
    back[0] = recv[0, 0:12, :]
    a_all.wait_send()
    b_all = pltpu.make_async_remote_copy(
        src_ref=mom_b.at[pl.ds(1, 15)], dst_ref=mom_b.at[pl.ds(1, 15)], send_sem=mom_sem.at[2], recv_sem=mom_sem.at[3],
        device_id=(lax.rem(d + 1, 16), s), device_id_type=MESH)
    b_all.wait()
    total_ref[...] = jnp.sum(mom_b[...], 0)
    pltpu.make_async_remote_copy(
        src_ref=stage.at[pl.ds(1, PEERS - 1)], dst_ref=recv.at[pl.ds(1, PEERS - 1)], send_sem=out_send,
        recv_sem=out_recv.at[0], device_id=shifted(d, s, 1, 1), device_id_type=MESH).wait_send()
    pltpu.make_async_remote_copy(
        src_ref=back.at[pl.ds(1, PEERS - 1)], dst_ref=back.at[pl.ds(1, PEERS - 1)], send_sem=back_send,
        recv_sem=back_recv, device_id=shifted(d, s, 1, 1), device_id_type=MESH).wait()
    back_ref[...] = back[...]


def run_exchange(near_of, live, send_flat, segments, mom):
    vm = pl.BlockSpec(memory_space=pltpu.VMEM)
    sm = pl.BlockSpec(memory_space=pltpu.SMEM)
    dma = pltpu.SemaphoreType.DMA
    return pl.pallas_call(
        exchange,
        out_shape=(
            jax.ShapeDtypeStruct((PEERS, 16, 128), f32),
            jax.ShapeDtypeStruct((PEERS, 12, 128), f32),
            jax.ShapeDtypeStruct((8, 128), f32),
        ),
        in_specs=[sm, sm, sm, pl.BlockSpec(memory_space=pl.ANY), vm],
        out_specs=(vm, vm, vm),
        scratch_shapes=[
            pltpu.VMEM((128, 9, 128), f32),
            pltpu.VMEM((PEERS, 36, 128), f32),
            pltpu.VMEM((PEERS, 36, 128), f32),
            pltpu.VMEM((PEERS, 12, 128), f32),
            pltpu.VMEM((128, 128, 128), bf16),
            pltpu.VMEM((128, 384, 128), f32),
            pltpu.VMEM((8 * (K + 8), 128), f32),
            pltpu.VMEM((GROUP, 8 * FROWS, 128), f32),
            pltpu.VMEM((GROUP, 128, 128), f32),
            pltpu.VMEM((8, 8, 128), f32),
            pltpu.VMEM((16, 8, 128), f32),
            dma(()),
            dma(()),
            dma((PEERS // GROUP,)),
            dma(()),
            dma(()),
            dma((4,)),
            pltpu.SemaphoreType.REGULAR,
        ],
        compiler_params=pltpu.CompilerParams(
            collective_id=0, has_side_effects=True, vmem_limit_bytes=58 << 20
        ),
    )(near_of, live, send_flat, segments, mom)


def collect(near_ref, send_ref, nraw, back, seg, out, acc, accf):
    d = lax.axis_index("dom")
    s = lax.axis_index("sub")
    acc[...] = jnp.zeros_like(acc)
    accf[...] = jnp.zeros_like(accf)

    def add(j, carry):
        nd, ns = shifted(d, s, j, -1)
        fd, fs = shifted(d, s, j, 1)
        for c in range(CAP):
            n = near_ref[(nd * 8 + ns) * CAP + c]
            acc[n] += nraw[j, 4 * c : 4 * c + 4, :]
            t = send_ref[(fd * 8 + fs) * CAP + c]
            accf[t, 0:3, :] += back[j, pl.ds(c, 3, stride=CAP), :]
        return carry

    lax.fori_loop(0, PEERS, add, 0)

    def finish(t, carry):
        out[t] = seg[t, 0:3, :] * acc[t, 3:4, :] - acc[t, 0:3, :] + accf[t, 0:3, :]
        return carry

    lax.fori_loop(0, 128, finish, 0)


def run_collect(near_of, send_flat, nraw, back, segments):
    vm = pl.BlockSpec(memory_space=pltpu.VMEM)
    sm = pl.BlockSpec(memory_space=pltpu.SMEM)
    return pl.pallas_call(
        collect,
        out_shape=jax.ShapeDtypeStruct((128, 3, 128), f32),
        in_specs=[sm, sm, vm, vm, vm],
        out_specs=vm,
        scratch_shapes=[pltpu.VMEM((128, 4, 128), f32), pltpu.VMEM((128, 4, 128), f32)],
        compiler_params=pltpu.CompilerParams(vmem_limit_bytes=32 << 20),
    )(near_of, send_flat, nraw, back, segments)


def far_field(segments, tile_cell, moment_sums, total_segments):
    moments = moment_sums.reshape(NCELL, 3, 3) / jnp.sqrt(jnp.float32(total_segments))
    moments = 0.5 * (moments + jnp.transpose(moments, (0, 2, 1)))
    cells = jnp.arange(NCELL).astype(jnp.float32)
    weights = 8.0 / (8.0 + jnp.abs(cells[:, None] - cells[None, :]))
    stress = jnp.dot(weights, moments.reshape(NCELL, 9), precision=lax.Precision.HIGHEST)
    onehot = (tile_cell[:, None] == jnp.arange(NCELL)[None, :]).astype(jnp.float32)
    tile_stress = jnp.dot(onehot, stress, precision=lax.Precision.HIGHEST).reshape(-1, 3, 3)
    traction = jnp.sum(tile_stress[:, :, :, None] * segments[:, None, 3:6, :], axis=2)
    lines = segments[:, 6:9, :]
    return jnp.stack(
        [
            traction[:, 1] * lines[:, 2] - traction[:, 2] * lines[:, 1],
            traction[:, 2] * lines[:, 0] - traction[:, 0] * lines[:, 2],
            traction[:, 0] * lines[:, 1] - traction[:, 1] * lines[:, 0],
        ],
        axis=1,
    )


def local_moments(segments, tile_cell):
    outer = jnp.sum(segments[:, 3:6, None, :] * segments[:, None, 6:9, :], axis=3).reshape(-1, 9)
    onehot = (jnp.arange(NCELL)[:, None] == tile_cell[None, :]).astype(jnp.float32)
    return jnp.dot(onehot, outer, precision=lax.Precision.HIGHEST)


def on_device(segments, send_tiles, pair_local, pair_remote, pair_count, tile_cell):
    width = segments.shape[2]
    slots = pair_remote.shape[1]
    here = pair_remote[0][None, :] == jnp.arange(slots, dtype=jnp.int32)[:, None]
    alive = (jnp.arange(slots) < pair_count[0]).astype(jnp.int32)
    code = jnp.sum(jnp.where(here, (pair_local[0] + 128 * alive)[None, :], 0), axis=1)
    near_of = lax.rem(code, 128)
    live = lax.div(code, 128).astype(f32)
    send_flat = send_tiles.reshape(-1)
    mom = local_moments(segments, tile_cell).reshape(-1)
    mom = jnp.concatenate([mom, jnp.zeros((1024 - mom.shape[0],), f32)]).reshape(8, 128)
    nraw, back, total = run_exchange(near_of, live, send_flat, segments, mom)
    pair_forces = run_collect(near_of, send_flat, nraw, back, segments)
    moment_sums = total.reshape(-1)[: NCELL * 9].reshape(NCELL, 9)
    total_segments = segments.shape[0] * width * PEERS
    return pair_forces + far_field(segments, tile_cell, moment_sums, total_segments)


def solution(mesh):
    in_specs = (
        P(("dom", "sub"), None, None),
        P(("dom", "sub"), None, None),
        P(("dom", "sub"), None),
        P(("dom", "sub"), None),
        P(("dom", "sub")),
        P(("dom", "sub")),
    )
    out_specs = P(("dom", "sub"), None, None)
    return jax.shard_map(
        on_device, mesh=mesh, in_specs=in_specs, out_specs=out_specs, check_vma=False
    )
```

```python
import math

import jax
import jax.numpy as jnp
from jax import lax
from jax.experimental import pallas as pl
from jax.experimental.pallas import tpu as pltpu
from jax.sharding import PartitionSpec as P

NCELL = 64
CAP = 4
PEERS = 128
MESH = pl.DeviceIdType.MESH
f32 = jnp.float32
bf16 = jnp.bfloat16

GROUP = 8
KNUM = 48
KDIST = 32
K = KNUM + KDIST
FROWS = K + 16
NT = (((1,), (1,)), ((), ()))
EXACT = lax.Precision.HIGHEST


def top(v):
    return v.astype(bf16).astype(f32)


def split2(v):
    h = top(v)
    return h, v - h


def split3(v):
    h = top(v)
    r = v - h
    m = top(r)
    return h, m, r - m


def near_rows(x, b, l):
    vals = list(b) + [b[i] * l[j] for i in range(3) for j in range(3)]
    hl = [split2(v) for v in vals]
    zero = jnp.zeros_like(x[0])
    one = zero + 1.0
    num = [h for h, _ in hl] + [h for h, _ in hl] + [lo for _, lo in hl]
    num += [zero] * (KNUM - 36)
    xs = [split3(v) for v in x]
    hi, mid, low = [[s[i] for s in xs] for i in range(3)]
    q = split3(x[0] * x[0] + x[1] * x[1] + x[2] * x[2] + 0.25)
    dist = hi + hi + mid + hi + low + mid + list(q) + [one] * 3
    dist += [zero] * (KDIST - 24)
    return num + dist


def far_rows(x, b, l):
    vals = list(b) + [l[i] * b[j] for i in range(3) for j in range(3)]
    hl = [split2(v) for v in vals]
    zero = jnp.zeros_like(x[0])
    one = zero + 1.0
    num = [h for h, _ in hl] + [lo for _, lo in hl] + [h for h, _ in hl]
    num += [zero] * (KNUM - 36)
    xs = [split3(v) for v in x]
    hi, mid, low = [[s[i] for s in xs] for i in range(3)]
    q = split3(x[0] * x[0] + x[1] * x[1] + x[2] * x[2])
    neg = lambda rows: [-2.0 * v for v in rows]
    nh, nm, nl = neg(hi), neg(mid), neg(low)
    dist = nh + nm + nh + nl + nh + nm + [one] * 3 + list(q)
    dist += [zero] * (KDIST - 24)
    rest = [v - h for v, h in zip(x, hi)]
    sums = hi + [one] + [zero] * 4 + rest + [zero] * 5
    return num + dist + sums


def put(scr, rows):
    for f, v in enumerate(rows):
        scr[8 * f : 8 * f + 8, :] = v


def prepare_near(seg, nft, spread, scr):
    k = lax.broadcasted_iota(jnp.int32, (K, 384), 0) - KNUM
    a = lax.broadcasted_iota(jnp.int32, (K, 384), 1) // 128
    pick = (k == a) | (k == a + 6) | (k == a + 12)
    pick = jnp.where(pick, 1.0, 0.0).astype(bf16)

    def body(g, carry):
        tiles = pl.ds(pl.multiple_of(g * 8, 8), 8)
        comp = [seg[i, tiles, :] for i in range(9)]
        put(scr, near_rows(comp[0:3], comp[3:6], comp[6:9]))
        for c in range(8):
            feat = scr[pl.ds(c, K, stride=8), :]
            feat = jnp.concatenate([feat, jnp.zeros((128 - K, 128), f32)], 0).T.astype(bf16)
            nft[g * 8 + c] = feat
            wide = jnp.dot(feat[:, :K], pick, preferred_element_type=f32)
            for i in range(3):
                spread[g * 8 + c, 128 * i : 128 * i + 128, :] = wide[:, 128 * i : 128 * i + 128]
        return carry

    lax.fori_loop(0, 16, body, 0)
    lane = lax.broadcasted_iota(jnp.int32, (128, 128), 1)
    nft[128] = jnp.where(lane == KNUM + 18, 1.0, 0.0).astype(bf16)
    spread[128] = jnp.zeros((384, 128), f32)


def block(comp, nears, nft, spread, scr, part):
    x, b, l = comp[0:3], comp[3:6], comp[6:9]
    put(scr, far_rows(x, b, l))
    near_parts = []
    zn = jnp.zeros((KNUM, 128), bf16)
    zd = jnp.zeros((KDIST, 128), bf16)
    for c in range(8):
        feat = scr[pl.ds(c, K, stride=8), :].astype(bf16)
        xf = scr[pl.ds(8 * K + c, 16, stride=8), :].astype(bf16)
        right = jnp.concatenate(
            [
                jnp.concatenate([feat[:KNUM], zn], 1),
                jnp.concatenate([zd, feat[KNUM:]], 1),
            ],
            0,
        )
        n = nears[c]
        both = jnp.dot(nft[n][:, :K], right, preferred_element_type=f32)
        inv = lax.rsqrt(both[:, 128:])
        coup = both[:, :128] * (inv * inv * inv)
        hi = coup.astype(bf16)
        lo = (coup - hi.astype(f32)).astype(bf16)
        sn = lax.dot_general(
            jnp.concatenate([xf, xf], 1),
            jnp.concatenate([hi, lo], 1),
            NT,
            preferred_element_type=f32,
        )
        near_parts.append(sn[0:8] + sn[8:16])
        acc = [None] * 4
        for i in range(16):
            cv = coup[8 * i : 8 * i + 8]
            for a in range(3):
                t = cv * spread[n, 128 * a + 8 * i : 128 * a + 8 * i + 8, :]
                acc[a] = t if acc[a] is None else acc[a] + t
            acc[3] = cv if acc[3] is None else acc[3] + cv
        for a in range(4):
            part[64 * a + 8 * c : 64 * a + 8 * c + 8, :] = acc[a]
    sums = []
    for a in range(4):
        s = part[pl.ds(64 * a, 8, stride=8), :]
        for i in range(1, 8):
            s = s + part[pl.ds(64 * a + i, 8, stride=8), :]
        sums.append(s)
    far = [x[a] * sums[3] - sums[a] for a in range(3)]
    return far, near_parts


def shifted(d, s, j, sign):
    k = (j * 37) & 127
    dx, dz, dy = k >> 5, (k >> 3) & 3, (k >> 1) & 3
    if sign < 0:
        dx, dz, dy = 4 - dx, 4 - dz, 4 - dy
    x = ((d >> 2) + dx) & 3
    z = ((d & 3) + dz) & 3
    y = ((s >> 1) + dy) & 3
    c = ((s & 1) + (k & 1)) & 1
    return x * 4 + z, y * 2 + c


def exchange(
    send_smem, seg_hbm, send_ref, local_ref, remote_ref, count_ref, cell_ref,
    out_ref,
    seg, tiles, stage, recv, back, nraw, nft, spread, nscr, scr, part, mom, mom_a, mom_b, nrow, near_smem,
    seg_sem, out_send, out_recv, back_send, back_recv, mom_sem, row_sem, stage_sem,
):
    d = lax.axis_index("dom")
    s = lax.axis_index("sub")
    me = d * 8 + s
    barrier = pltpu.get_barrier_semaphore()
    for k in range(1, 8):
        pl.semaphore_signal(barrier, inc=1, device_id=(d, (s + k) & 7), device_id_type=MESH)
    for k in range(1, 16):
        pl.semaphore_signal(barrier, inc=1, device_id=((d + k) & 15, s), device_id_type=MESH)
    load = pltpu.make_async_copy(seg_hbm, seg, seg_sem)
    load.start()

    remote = remote_ref[...]
    slot = (remote & 3) * 128 + (remote >> 2)
    pair = lax.broadcasted_iota(jnp.int32, (1, 512), 1)
    value = jnp.where(pair < count_ref[0], local_ref[...], 128).astype(f32).astype(bf16)
    value = jnp.broadcast_to(value, (16, 512))
    rows = lax.broadcasted_iota(jnp.int32, (128, 512), 0)
    for c in range(CAP):
        here = jnp.where(rows + 128 * c == slot, 1.0, 0.0).astype(bf16)
        row = lax.dot_general(value, here, NT, preferred_element_type=f32)
        nrow[c : c + 1, :] = jnp.clip(row[0:1].astype(jnp.int32), 0, 128)
    nrow[4:8, :] = jnp.zeros((4, 128), jnp.int32)
    to_smem = pltpu.make_async_copy(nrow, near_smem, row_sem)
    to_smem.start()

    load.wait()
    for g in range(16):
        for a in range(9):
            tiles[8 * g : 8 * g + 8, a, :] = seg[a, 8 * g : 8 * g + 8, :]

    def gather(j, carry):
        td, ts = shifted(d, s, j, 1)
        there = td * 8 + ts
        for c in range(CAP):
            stage[j, 9 * c : 9 * c + 9, :] = tiles[send_smem[c, there]]
        return carry

    lax.fori_loop(0, PEERS, gather, 0)
    recv[0:36, :] = stage[0]

    lane = lax.broadcasted_iota(jnp.int32, (128, 128), 1)
    cells = lax.broadcasted_iota(jnp.int32, (128, 128), 0)
    onehot = jnp.where(cells == cell_ref[...], 1.0, 0.0)
    outer = jnp.zeros((128, 128), f32)
    for a in range(3):
        for b in range(3):
            total = jnp.sum(seg[3 + a] * seg[6 + b], axis=1, keepdims=True)
            outer = jnp.where(lane == 3 * a + b, total, outer)
    mom[...] = jnp.dot(onehot, outer, precision=EXACT, preferred_element_type=f32).T[0:16]
    mom_a[0] = mom[...]

    pl.semaphore_wait(barrier, 22)
    for k in range(1, 8):
        pl.semaphore_signal(stage_sem, inc=1, device_id=(d, (s + k) & 7), device_id_type=MESH)
    pl.semaphore_wait(stage_sem, 7)

    for k in range(1, 8):
        pltpu.make_async_remote_copy(
            src_ref=mom, dst_ref=mom_a.at[k], send_sem=mom_sem.at[0], recv_sem=mom_sem.at[1],
            device_id=(d, (s + k) & 7), device_id_type=MESH).start()

    def send(j, carry):
        pltpu.make_async_remote_copy(
            src_ref=stage.at[j], dst_ref=recv.at[pl.ds(pl.multiple_of(j * 40, 8), 36)],
            send_sem=out_send, recv_sem=out_recv.at[j // GROUP],
            device_id=shifted(d, s, j, 1), device_id_type=MESH).start()
        return carry

    lax.fori_loop(1, PEERS, send, 0)
    prepare_near(seg, nft, spread, nscr)

    a_all = pltpu.make_async_remote_copy(
        src_ref=mom_a.at[pl.ds(1, 7)], dst_ref=mom_a.at[pl.ds(1, 7)], send_sem=mom_sem.at[0], recv_sem=mom_sem.at[1],
        device_id=(d, (s + 1) & 7), device_id_type=MESH)
    a_all.wait()
    mom_b[0] = jnp.sum(mom_a[...], 0)
    for k in range(1, 16):
        pltpu.make_async_remote_copy(
            src_ref=mom_b.at[0], dst_ref=mom_b.at[k], send_sem=mom_sem.at[2], recv_sem=mom_sem.at[3],
            device_id=((d + k) & 15, s), device_id_type=MESH).start()
    to_smem.wait()

    def wait_blocks(count, g):
        pltpu.make_async_remote_copy(
            src_ref=stage.at[pl.ds(0, count)], dst_ref=stage.at[pl.ds(0, count)],
            send_sem=out_send, recv_sem=out_recv.at[g],
            device_id=shifted(d, s, 1, 1), device_id_type=MESH).wait_recv()

    low = lax.broadcasted_iota(jnp.int32, (8, 128), 0) < CAP

    def work(g, carry):
        @pl.when(g == 0)
        def _():
            wait_blocks(GROUP - 1, 0)

        @pl.when(g > 0)
        def _():
            wait_blocks(GROUP, g)

        for u in range(GROUP // 2):
            j = g * GROUP + 2 * u
            first = pl.multiple_of(j * 40, 8)
            comp = []
            for a in range(9):
                even = recv[pl.ds(first + a, 8, stride=9), :]
                odd = recv[pl.ds(first + 4 + a, 8, stride=9), :]
                comp.append(jnp.where(low, even, odd))
            who = []
            for v in range(2):
                td, ts = shifted(d, s, j + v, -1)
                who.append(td * 8 + ts)
            nears = [jnp.clip(near_smem[c, who[v]], 0, 128) for v in range(2) for c in range(CAP)]
            far, near = block(comp, nears, nft, spread, scr.at[u], part.at[u])
            for v in range(2):
                for a in range(3):
                    recv[pl.ds(first + 40 * v + CAP * a, CAP), :] = far[a][CAP * v : CAP * v + CAP]
                for c in range(CAP):
                    nraw[pl.ds(pl.multiple_of(who[v] * 16, 16) + 4 * c, 4), :] = near[CAP * v + c][0:4]

        for u in range(GROUP):
            j = g * GROUP + u

            @pl.when(j > 0)
            def _():
                pltpu.make_async_remote_copy(
                    src_ref=recv.at[pl.ds(pl.multiple_of(j * 40, 8), 12)],
                    dst_ref=back.at[pl.ds(pl.multiple_of(me * 16, 16), 12)],
                    send_sem=back_send, recv_sem=back_recv,
                    device_id=shifted(d, s, j, -1), device_id_type=MESH).start()

        return carry

    lax.fori_loop(0, PEERS // GROUP, work, 0)
    back[pl.ds(pl.multiple_of(me * 16, 16), 12), :] = recv[0:12, :]

    b_all = pltpu.make_async_remote_copy(
        src_ref=mom_b.at[pl.ds(1, 15)], dst_ref=mom_b.at[pl.ds(1, 15)], send_sem=mom_sem.at[2], recv_sem=mom_sem.at[3],
        device_id=((d + 1) & 15, s), device_id_type=MESH)
    b_all.wait()
    sums = jnp.sum(mom_b[...], 0)
    scale = 0.5 / math.sqrt(PEERS * 128 * 128)
    sym = [(sums[3 * a + b : 3 * a + b + 1] + sums[3 * b + a : 3 * b + a + 1]) * scale for a in range(3) for b in range(3)]
    moments = jnp.concatenate(sym + [jnp.zeros((128 - 9, 128), f32)], 0).T
    rows = lax.broadcasted_iota(jnp.int32, (128, 128), 0)
    lanes = lax.broadcasted_iota(jnp.int32, (128, 128), 1)
    weights = 8.0 / (8.0 + jnp.abs(rows - lanes).astype(f32))
    stress = jnp.dot(weights, moments, precision=EXACT, preferred_element_type=f32)
    onehot = jnp.where(rows == cell_ref[...], 1.0, 0.0).T
    ts = jnp.dot(onehot, stress, precision=EXACT, preferred_element_type=f32)

    pick = jnp.concatenate([jnp.where(rows == nrow[c : c + 1, :], 1.0, 0.0).astype(bf16) for c in range(CAP)], 1)

    def gathered(ref, a, which):
        v = jnp.concatenate([ref[pl.ds(4 * c + a if which else 4 * a + c, 128, stride=16), :] for c in range(CAP)], 0)
        hi = v.astype(bf16)
        lo = (v - hi.astype(f32)).astype(bf16)
        return jnp.concatenate([hi, lo], 1)

    near = []
    for a in range(4):
        both = jnp.dot(pick, gathered(nraw, a, True), preferred_element_type=f32)
        near.append(both[:, :128] + both[:, 128:])
    for g in range(16):
        r = slice(8 * g, 8 * g + 8)
        pull = []
        for k in range(3):
            parts = [jnp.broadcast_to(ts[r, 3 * k + m : 3 * k + m + 1], (8, 128)) * seg[3 + m, r, :] for m in range(3)]
            pull.append(parts[0] + parts[1] + parts[2])
        line = [seg[6 + m, r, :] for m in range(3)]
        for a in range(3):
            p, q = (a + 1) % 3, (a + 2) % 3
            field = pull[p] * line[q] - pull[q] * line[p]
            out_ref[a, r, :] = seg[a, r, :] * near[3][r] - near[a][r] + field

    pltpu.make_async_remote_copy(
        src_ref=stage.at[pl.ds(1, PEERS - 1)], dst_ref=stage.at[pl.ds(1, PEERS - 1)], send_sem=out_send,
        recv_sem=out_recv.at[0], device_id=shifted(d, s, 1, 1), device_id_type=MESH).wait_send()
    pltpu.make_async_remote_copy(
        src_ref=stage.at[pl.ds(1, PEERS - 1), pl.ds(0, 12)], dst_ref=stage.at[pl.ds(1, PEERS - 1), pl.ds(0, 12)],
        send_sem=back_send, recv_sem=back_recv, device_id=shifted(d, s, 1, 1), device_id_type=MESH).wait()

    pick = jnp.concatenate([jnp.where(rows == send_ref[c : c + 1, :], 1.0, 0.0).astype(bf16) for c in range(CAP)], 1)
    for a in range(3):
        both = jnp.dot(pick, gathered(back, a, False), preferred_element_type=f32)
        out_ref[a] += both[:, :128] + both[:, 128:]


def on_device(segments, send_tiles, pair_local, pair_remote, pair_count, tile_cell):
    vm = pl.BlockSpec(memory_space=pltpu.VMEM)
    sm = pl.BlockSpec(memory_space=pltpu.SMEM)
    dma = pltpu.SemaphoreType.DMA
    slots = send_tiles[0].T
    forces = pl.pallas_call(
        exchange,
        out_shape=jax.ShapeDtypeStruct((3, 128, 128), f32),
        in_specs=[sm, pl.BlockSpec(memory_space=pl.ANY), vm, vm, vm, sm, vm],
        out_specs=vm,
        scratch_shapes=[
            pltpu.VMEM((9, 128, 128), f32),
            pltpu.VMEM((128, 9, 128), f32),
            pltpu.VMEM((PEERS, 36, 128), f32),
            pltpu.VMEM((PEERS * 40, 128), f32),
            pltpu.VMEM((PEERS * 16, 128), f32),
            pltpu.VMEM((PEERS * 16, 128), f32),
            pltpu.VMEM((129, 128, 128), bf16),
            pltpu.VMEM((129, 384, 128), f32),
            pltpu.VMEM((8 * K, 128), f32),
            pltpu.VMEM((GROUP // 2, 8 * FROWS, 128), f32),
            pltpu.VMEM((GROUP // 2, 256, 128), f32),
            pltpu.VMEM((16, 128), f32),
            pltpu.VMEM((8, 16, 128), f32),
            pltpu.VMEM((16, 16, 128), f32),
            pltpu.VMEM((8, 128), jnp.int32),
            pltpu.SMEM((8, 128), jnp.int32),
            dma(()),
            dma(()),
            dma((PEERS // GROUP,)),
            dma(()),
            dma(()),
            dma((4,)),
            dma(()),
            pltpu.SemaphoreType.REGULAR,
        ],
        compiler_params=pltpu.CompilerParams(
            collective_id=0, has_side_effects=True, vmem_limit_bytes=58 << 20
        ),
    )(
        slots,
        segments.transpose(1, 0, 2),
        slots,
        pair_local,
        pair_remote,
        pair_count,
        tile_cell.reshape(1, -1),
    )
    return forces.transpose(1, 0, 2)


def solution(mesh):
    in_specs = (
        P(("dom", "sub"), None, None),
        P(("dom", "sub"), None, None),
        P(("dom", "sub"), None),
        P(("dom", "sub"), None),
        P(("dom", "sub")),
        P(("dom", "sub")),
    )
    out_specs = P(("dom", "sub"), None, None)
    return jax.shard_map(
        on_device, mesh=mesh, in_specs=in_specs, out_specs=out_specs, check_vma=False
    )
```

```python
import math

import jax
import jax.numpy as jnp
from jax import lax
from jax.experimental import pallas as pl
from jax.experimental.pallas import tpu as pltpu
from jax.sharding import PartitionSpec as P

NCELL = 64
CAP = 4
PEERS = 128
MESH = pl.DeviceIdType.MESH
f32 = jnp.float32
bf16 = jnp.bfloat16

GROUP = 8
KNUM = 48
KDIST = 32
K = KNUM + KDIST
FROWS = K + 16
NT = (((1,), (1,)), ((), ()))
EXACT = lax.Precision.HIGHEST


def top(v):
    return v.astype(bf16).astype(f32)


def split2(v):
    h = top(v)
    return h, v - h


def split3(v):
    h = top(v)
    r = v - h
    m = top(r)
    return h, m, r - m


def near_rows(x, b, l):
    vals = list(b) + [b[i] * l[j] for i in range(3) for j in range(3)]
    hl = [split2(v) for v in vals]
    zero = jnp.zeros_like(x[0])
    one = zero + 1.0
    num = [h for h, _ in hl] + [h for h, _ in hl] + [lo for _, lo in hl]
    num += [zero] * (KNUM - 36)
    xs = [split3(v) for v in x]
    hi, mid, low = [[s[i] for s in xs] for i in range(3)]
    q = split3(x[0] * x[0] + x[1] * x[1] + x[2] * x[2] + 0.25)
    dist = hi + hi + mid + hi + low + mid + list(q) + [one] * 3
    dist += [zero] * (KDIST - 24)
    return num + dist


def far_rows(x, b, l):
    vals = list(b) + [l[i] * b[j] for i in range(3) for j in range(3)]
    hl = [split2(v) for v in vals]
    zero = jnp.zeros_like(x[0])
    one = zero + 1.0
    num = [h for h, _ in hl] + [lo for _, lo in hl] + [h for h, _ in hl]
    num += [zero] * (KNUM - 36)
    xs = [split3(v) for v in x]
    hi, mid, low = [[s[i] for s in xs] for i in range(3)]
    q = split3(x[0] * x[0] + x[1] * x[1] + x[2] * x[2])
    neg = lambda rows: [-2.0 * v for v in rows]
    nh, nm, nl = neg(hi), neg(mid), neg(low)
    dist = nh + nm + nh + nl + nh + nm + [one] * 3 + list(q)
    dist += [zero] * (KDIST - 24)
    rest = [v - h for v, h in zip(x, hi)]
    sums = hi + [one] + [zero] * 4 + rest + [zero] * 5
    return num + dist + sums


def put(scr, rows):
    for f, v in enumerate(rows):
        scr[8 * f : 8 * f + 8, :] = v


def prepare_near(seg, nft, spread, scr):
    k = lax.broadcasted_iota(jnp.int32, (K, 384), 0) - KNUM
    a = lax.broadcasted_iota(jnp.int32, (K, 384), 1) // 128
    pick = (k == a) | (k == a + 6) | (k == a + 12)
    pick = jnp.where(pick, 1.0, 0.0).astype(bf16)

    def body(g, carry):
        tiles = pl.ds(pl.multiple_of(g * 8, 8), 8)
        comp = [seg[i, tiles, :] for i in range(9)]
        put(scr, near_rows(comp[0:3], comp[3:6], comp[6:9]))
        for c in range(8):
            feat = scr[pl.ds(c, K, stride=8), :]
            feat = jnp.concatenate([feat, jnp.zeros((128 - K, 128), f32)], 0).T.astype(bf16)
            nft[g * 8 + c] = feat
            wide = jnp.dot(feat[:, :K], pick, preferred_element_type=f32)
            for i in range(3):
                spread[g * 8 + c, 128 * i : 128 * i + 128, :] = wide[:, 128 * i : 128 * i + 128]
        return carry

    lax.fori_loop(0, 16, body, 0)
    lane = lax.broadcasted_iota(jnp.int32, (128, 128), 1)
    nft[128] = jnp.where(lane == KNUM + 18, 1.0, 0.0).astype(bf16)
    spread[128] = jnp.zeros((384, 128), f32)


def block(comp, nears, nft, spread, scr, part):
    x, b, l = comp[0:3], comp[3:6], comp[6:9]
    put(scr, far_rows(x, b, l))
    near_parts = []
    zn = jnp.zeros((KNUM, 128), bf16)
    zd = jnp.zeros((KDIST, 128), bf16)
    for c in range(8):
        feat = scr[pl.ds(c, K, stride=8), :].astype(bf16)
        xf = scr[pl.ds(8 * K + c, 16, stride=8), :].astype(bf16)
        right = jnp.concatenate(
            [
                jnp.concatenate([feat[:KNUM], zn], 1),
                jnp.concatenate([zd, feat[KNUM:]], 1),
            ],
            0,
        )
        n = nears[c]
        both = jnp.dot(nft[n][:, :K], right, preferred_element_type=f32)
        inv = lax.rsqrt(both[:, 128:])
        coup = both[:, :128] * (inv * inv * inv)
        hi = coup.astype(bf16)
        lo = (coup - hi.astype(f32)).astype(bf16)
        sn = lax.dot_general(
            jnp.concatenate([xf, xf], 1),
            jnp.concatenate([hi, lo], 1),
            NT,
            preferred_element_type=f32,
        )
        near_parts.append(sn[0:8] + sn[8:16])
        acc = [None] * 4
        for i in range(16):
            cv = coup[8 * i : 8 * i + 8]
            for a in range(3):
                t = cv * spread[n, 128 * a + 8 * i : 128 * a + 8 * i + 8, :]
                acc[a] = t if acc[a] is None else acc[a] + t
            acc[3] = cv if acc[3] is None else acc[3] + cv
        for a in range(4):
            part[64 * a + 8 * c : 64 * a + 8 * c + 8, :] = acc[a]
    sums = []
    for a in range(4):
        s = part[pl.ds(64 * a, 8, stride=8), :]
        for i in range(1, 8):
            s = s + part[pl.ds(64 * a + i, 8, stride=8), :]
        sums.append(s)
    far = [x[a] * sums[3] - sums[a] for a in range(3)]
    return far, near_parts


FIRST = 23


def shifted(d, s, j, sign):
    k = (j * 37) & 127
    dx, dz, dy, dc = k >> 5, (k >> 3) & 3, (k >> 1) & 3, k & 1
    if sign < 0:
        dx, dz, dy = 4 - dx, 4 - dz, 4 - dy
    x = ((d >> 2) + dx) & 3
    z = ((d & 3) + dz) & 3
    y = ((s >> 1) + dy) & 3
    c = ((s & 1) + dc) & 1
    return x * 4 + z, y * 2 + c


def exchange(
    seg_hbm, send_hbm, local_hbm, remote_hbm, count_hbm, cell_hbm,
    out_ref,
    send_smem, send_ref, local_ref, remote_ref, count_ref, cell_ref,
    seg, tiles, stage, recv, back, nraw, nft, spread, nscr, scr, part, mom, mom_a, mom_b, nrow, near_smem,
    seg_sem, out_send, out_recv, back_send, back_recv, mom_sem, row_sem, arg_sem, stage_sem,
):
    d = lax.axis_index("dom")
    s = lax.axis_index("sub")
    me = d * 8 + s
    barrier = pltpu.get_barrier_semaphore()
    for k in range(1, 8):
        pl.semaphore_signal(barrier, inc=1, device_id=(d, (s + k) & 7), device_id_type=MESH)
    for k in range(1, 16):
        pl.semaphore_signal(barrier, inc=1, device_id=((d + k) & 15, s), device_id_type=MESH)
    load = pltpu.make_async_copy(seg_hbm, seg, seg_sem)
    load.start()
    moves = [
        (send_hbm, send_smem), (local_hbm, local_ref), (remote_hbm, remote_ref),
        (count_hbm, count_ref), (cell_hbm, cell_ref), (send_hbm, send_ref),
    ]
    moves = [pltpu.make_async_copy(a, b, arg_sem.at[i]) for i, (a, b) in enumerate(moves)]
    for move in moves:
        move.start()
    load.wait()
    for g in range(16):
        for a in range(9):
            tiles[8 * g : 8 * g + 8, a, :] = seg[a, 8 * g : 8 * g + 8, :]
    for move in moves:
        move.wait()

    def gather(j):
        td, ts = shifted(d, s, j, 1)
        there = td * 8 + ts
        for c in range(CAP):
            stage[j, 9 * c : 9 * c + 9, :] = tiles[send_smem[c, there]]
        return td, ts

    def send(j, carry):
        partner = gather(j)
        pltpu.make_async_remote_copy(
            src_ref=stage.at[j], dst_ref=recv.at[pl.ds(pl.multiple_of(j * 40, 8), 36)],
            send_sem=out_send, recv_sem=out_recv.at[j // GROUP],
            device_id=partner, device_id_type=MESH).start()
        return carry

    pl.semaphore_wait(barrier, 22)
    for k in range(1, 8):
        pl.semaphore_signal(stage_sem, inc=1, device_id=(d, (s + k) & 7), device_id_type=MESH)
    pl.semaphore_wait(stage_sem, 7)
    lax.fori_loop(1, FIRST, send, 0)

    lane = lax.broadcasted_iota(jnp.int32, (128, 128), 1)
    cells = lax.broadcasted_iota(jnp.int32, (128, 128), 0)
    onehot = jnp.where(cells == cell_ref[...], 1.0, 0.0)
    outer = jnp.zeros((128, 128), f32)
    for a in range(3):
        for b in range(3):
            total = jnp.sum(seg[3 + a] * seg[6 + b], axis=1, keepdims=True)
            outer = jnp.where(lane == 3 * a + b, total, outer)
    sums = jnp.dot(onehot, outer, precision=EXACT, preferred_element_type=f32).T
    last = jnp.concatenate([jnp.zeros((1, NCELL), f32), sums[8:9, :NCELL]], 1)
    mom[...] = sums[0:8] + jnp.concatenate([last, jnp.zeros((7, 128), f32)], 0)
    mom_a[0] = mom[...]
    for k in range(1, 8):
        pltpu.make_async_remote_copy(
            src_ref=mom, dst_ref=mom_a.at[k], send_sem=mom_sem.at[0], recv_sem=mom_sem.at[1],
            device_id=(d, (s + k) & 7), device_id_type=MESH).start()

    lax.fori_loop(FIRST, PEERS, send, 0)
    gather(0)
    recv[0:36, :] = stage[0]

    remote = remote_ref[...]
    slot = (remote & 3) * 128 + (remote >> 2)
    pair = lax.broadcasted_iota(jnp.int32, (1, 512), 1)
    value = jnp.where(pair < count_ref[0], local_ref[...], 128).astype(f32).astype(bf16)
    value = jnp.broadcast_to(value, (16, 512))
    rows = lax.broadcasted_iota(jnp.int32, (128, 512), 0)
    for c in range(CAP):
        here = jnp.where(rows + 128 * c == slot, 1.0, 0.0).astype(bf16)
        row = lax.dot_general(value, here, NT, preferred_element_type=f32)
        nrow[c : c + 1, :] = jnp.clip(row[0:1].astype(jnp.int32), 0, 128)
    nrow[4:8, :] = jnp.zeros((4, 128), jnp.int32)
    to_smem = pltpu.make_async_copy(nrow, near_smem, row_sem)
    to_smem.start()
    prepare_near(seg, nft, spread, nscr)

    a_all = pltpu.make_async_remote_copy(
        src_ref=mom_a.at[pl.ds(1, 7)], dst_ref=mom_a.at[pl.ds(1, 7)], send_sem=mom_sem.at[0], recv_sem=mom_sem.at[1],
        device_id=(d, (s + 1) & 7), device_id_type=MESH)
    a_all.wait()
    mom_b[0] = jnp.sum(mom_a[...], 0)
    for k in range(1, 16):
        pltpu.make_async_remote_copy(
            src_ref=mom_b.at[0], dst_ref=mom_b.at[k], send_sem=mom_sem.at[2], recv_sem=mom_sem.at[3],
            device_id=((d + k) & 15, s), device_id_type=MESH).start()
    to_smem.wait()

    def wait_blocks(count, g):
        pltpu.make_async_remote_copy(
            src_ref=stage.at[pl.ds(0, count)], dst_ref=stage.at[pl.ds(0, count)],
            send_sem=out_send, recv_sem=out_recv.at[g],
            device_id=shifted(d, s, 1, 1), device_id_type=MESH).wait_recv()

    low = lax.broadcasted_iota(jnp.int32, (8, 128), 0) < CAP

    def work(g, carry):
        @pl.when(g == 0)
        def _():
            wait_blocks(GROUP - 1, 0)

        @pl.when(g > 0)
        def _():
            wait_blocks(GROUP, g)

        for u in range(GROUP // 2):
            j = g * GROUP + 2 * u
            first = pl.multiple_of(j * 40, 8)
            comp = []
            for a in range(9):
                even = recv[pl.ds(first + a, 8, stride=9), :]
                odd = recv[pl.ds(first + 4 + a, 8, stride=9), :]
                comp.append(jnp.where(low, even, odd))
            who = []
            for v in range(2):
                td, ts = shifted(d, s, j + v, -1)
                who.append(td * 8 + ts)
            nears = [jnp.clip(near_smem[c, who[v]], 0, 128) for v in range(2) for c in range(CAP)]
            far, near = block(comp, nears, nft, spread, scr.at[u], part.at[u])
            for v in range(2):
                for a in range(3):
                    recv[pl.ds(first + 40 * v + CAP * a, CAP), :] = far[a][CAP * v : CAP * v + CAP]
                for c in range(CAP):
                    nraw[pl.ds(pl.multiple_of(who[v] * 16, 16) + 4 * c, 4), :] = near[CAP * v + c][0:4]

        for u in range(GROUP):
            j = g * GROUP + u

            @pl.when(j > 0)
            def _():
                pltpu.make_async_remote_copy(
                    src_ref=recv.at[pl.ds(pl.multiple_of(j * 40, 8), 12)],
                    dst_ref=back.at[pl.ds(pl.multiple_of(me * 16, 16), 12)],
                    send_sem=back_send, recv_sem=back_recv,
                    device_id=shifted(d, s, j, -1), device_id_type=MESH).start()

        return carry

    lax.fori_loop(0, PEERS // GROUP, work, 0)
    back[pl.ds(pl.multiple_of(me * 16, 16), 12), :] = recv[0:12, :]

    b_all = pltpu.make_async_remote_copy(
        src_ref=mom_b.at[pl.ds(1, 15)], dst_ref=mom_b.at[pl.ds(1, 15)], send_sem=mom_sem.at[2], recv_sem=mom_sem.at[3],
        device_id=((d + 1) & 15, s), device_id_type=MESH)
    b_all.wait()
    packed = jnp.sum(mom_b[...], 0)
    sums = [packed[r : r + 1, :NCELL] for r in range(8)] + [packed[0:1, NCELL:]]
    scale = 0.5 / math.sqrt(PEERS * 128 * 128)
    sym = [(sums[3 * a + b] + sums[3 * b + a]) * scale for a in range(3) for b in range(3)]
    sym = jnp.concatenate(sym + [jnp.zeros((128 - 9, NCELL), f32)], 0)
    moments = jnp.concatenate([sym, jnp.zeros((128, 128 - NCELL), f32)], 1).T
    rows = lax.broadcasted_iota(jnp.int32, (128, 128), 0)
    lanes = lax.broadcasted_iota(jnp.int32, (128, 128), 1)
    weights = 8.0 / (8.0 + jnp.abs(rows - lanes).astype(f32))
    stress = jnp.dot(weights, moments, precision=EXACT, preferred_element_type=f32)
    onehot = jnp.where(rows == cell_ref[...], 1.0, 0.0).T
    ts = jnp.dot(onehot, stress, precision=EXACT, preferred_element_type=f32)

    pick = jnp.concatenate([jnp.where(rows == nrow[c : c + 1, :], 1.0, 0.0).astype(bf16) for c in range(CAP)], 1)

    def gathered(ref, a, which):
        v = jnp.concatenate([ref[pl.ds(4 * c + a if which else 4 * a + c, 128, stride=16), :] for c in range(CAP)], 0)
        hi = v.astype(bf16)
        lo = (v - hi.astype(f32)).astype(bf16)
        return jnp.concatenate([hi, lo], 1)

    near = []
    for a in range(4):
        both = jnp.dot(pick, gathered(nraw, a, True), preferred_element_type=f32)
        near.append(both[:, :128] + both[:, 128:])
    for g in range(16):
        r = slice(8 * g, 8 * g + 8)
        pull = []
        for k in range(3):
            parts = [jnp.broadcast_to(ts[r, 3 * k + m : 3 * k + m + 1], (8, 128)) * seg[3 + m, r, :] for m in range(3)]
            pull.append(parts[0] + parts[1] + parts[2])
        line = [seg[6 + m, r, :] for m in range(3)]
        for a in range(3):
            p, q = (a + 1) % 3, (a + 2) % 3
            field = pull[p] * line[q] - pull[q] * line[p]
            out_ref[a, r, :] = seg[a, r, :] * near[3][r] - near[a][r] + field

    pltpu.make_async_remote_copy(
        src_ref=stage.at[pl.ds(1, PEERS - 1)], dst_ref=stage.at[pl.ds(1, PEERS - 1)], send_sem=out_send,
        recv_sem=out_recv.at[0], device_id=shifted(d, s, 1, 1), device_id_type=MESH).wait_send()
    pltpu.make_async_remote_copy(
        src_ref=stage.at[pl.ds(1, PEERS - 1), pl.ds(0, 12)], dst_ref=stage.at[pl.ds(1, PEERS - 1), pl.ds(0, 12)],
        send_sem=back_send, recv_sem=back_recv, device_id=shifted(d, s, 1, 1), device_id_type=MESH).wait()

    pick = jnp.concatenate([jnp.where(rows == send_ref[c : c + 1, :], 1.0, 0.0).astype(bf16) for c in range(CAP)], 1)
    for a in range(3):
        both = jnp.dot(pick, gathered(back, a, False), preferred_element_type=f32)
        out_ref[a] += both[:, :128] + both[:, 128:]


def on_device(segments, send_tiles, pair_local, pair_remote, pair_count, tile_cell):
    vm = pl.BlockSpec(memory_space=pltpu.VMEM)
    dma = pltpu.SemaphoreType.DMA
    slots = send_tiles[0].T
    forces = pl.pallas_call(
        exchange,
        out_shape=jax.ShapeDtypeStruct((3, 128, 128), f32),
        in_specs=[pl.BlockSpec(memory_space=pl.ANY)] * 6,
        out_specs=vm,
        scratch_shapes=[
            pltpu.SMEM((CAP, 128), jnp.int32),
            pltpu.VMEM((CAP, 128), jnp.int32),
            pltpu.VMEM((1, 512), jnp.int32),
            pltpu.VMEM((1, 512), jnp.int32),
            pltpu.SMEM((1,), jnp.int32),
            pltpu.VMEM((1, 128), jnp.int32),
            pltpu.VMEM((9, 128, 128), f32),
            pltpu.VMEM((128, 9, 128), f32),
            pltpu.VMEM((PEERS, 36, 128), f32),
            pltpu.VMEM((PEERS * 40, 128), f32),
            pltpu.VMEM((PEERS * 16, 128), f32),
            pltpu.VMEM((PEERS * 16, 128), f32),
            pltpu.VMEM((129, 128, 128), bf16),
            pltpu.VMEM((129, 384, 128), f32),
            pltpu.VMEM((8 * K, 128), f32),
            pltpu.VMEM((GROUP // 2, 8 * FROWS, 128), f32),
            pltpu.VMEM((GROUP // 2, 256, 128), f32),
            pltpu.VMEM((8, 128), f32),
            pltpu.VMEM((8, 8, 128), f32),
            pltpu.VMEM((16, 8, 128), f32),
            pltpu.VMEM((8, 128), jnp.int32),
            pltpu.SMEM((8, 128), jnp.int32),
            dma(()),
            dma(()),
            dma((PEERS // GROUP,)),
            dma(()),
            dma(()),
            dma((4,)),
            dma(()),
            dma((6,)),
            pltpu.SemaphoreType.REGULAR,
        ],
        compiler_params=pltpu.CompilerParams(
            collective_id=0, has_side_effects=True, vmem_limit_bytes=58 << 20
        ),
    )(
        segments.transpose(1, 0, 2),
        slots,
        pair_local,
        pair_remote,
        pair_count,
        tile_cell.reshape(1, -1),
    )
    return forces.transpose(1, 0, 2)


def solution(mesh):
    in_specs = (
        P(("dom", "sub"), None, None),
        P(("dom", "sub"), None, None),
        P(("dom", "sub"), None),
        P(("dom", "sub"), None),
        P(("dom", "sub")),
        P(("dom", "sub")),
    )
    out_specs = P(("dom", "sub"), None, None)
    return jax.shard_map(
        on_device, mesh=mesh, in_specs=in_specs, out_specs=out_specs, check_vma=False
    )
```

```python
import math

import jax
import jax.numpy as jnp
from jax import lax
from jax.experimental import pallas as pl
from jax.experimental.pallas import tpu as pltpu
from jax.sharding import PartitionSpec as P

NCELL = 64
CAP = 4
PEERS = 128
MESH = pl.DeviceIdType.MESH
f32 = jnp.float32
bf16 = jnp.bfloat16

GROUP = 8
KNUM = 48
KDIST = 32
K = KNUM + KDIST
FROWS = K + 16
NT = (((1,), (1,)), ((), ()))
EXACT = lax.Precision.HIGHEST


def top(v):
    return v.astype(bf16).astype(f32)


def split2(v):
    h = top(v)
    return h, v - h


def split3(v):
    h = top(v)
    r = v - h
    m = top(r)
    return h, m, r - m


def near_rows(x, b, l):
    vals = list(b) + [b[i] * l[j] for i in range(3) for j in range(3)]
    hl = [split2(v) for v in vals]
    zero = jnp.zeros_like(x[0])
    one = zero + 1.0
    num = [h for h, _ in hl] + [h for h, _ in hl] + [lo for _, lo in hl]
    num += [zero] * (KNUM - 36)
    xs = [split3(v) for v in x]
    hi, mid, low = [[s[i] for s in xs] for i in range(3)]
    q = split3(x[0] * x[0] + x[1] * x[1] + x[2] * x[2] + 0.25)
    dist = hi + hi + mid + hi + low + mid + list(q) + [one] * 3
    dist += [zero] * (KDIST - 24)
    return num + dist


def far_rows(x, b, l):
    vals = list(b) + [l[i] * b[j] for i in range(3) for j in range(3)]
    hl = [split2(v) for v in vals]
    zero = jnp.zeros_like(x[0])
    one = zero + 1.0
    num = [h for h, _ in hl] + [lo for _, lo in hl] + [h for h, _ in hl]
    num += [zero] * (KNUM - 36)
    xs = [split3(v) for v in x]
    hi, mid, low = [[s[i] for s in xs] for i in range(3)]
    q = split3(x[0] * x[0] + x[1] * x[1] + x[2] * x[2])
    neg = lambda rows: [-2.0 * v for v in rows]
    nh, nm, nl = neg(hi), neg(mid), neg(low)
    dist = nh + nm + nh + nl + nh + nm + [one] * 3 + list(q)
    dist += [zero] * (KDIST - 24)
    rest = [v - h for v, h in zip(x, hi)]
    sums = hi + [one] + [zero] * 4 + rest + [zero] * 5
    return num + dist + sums


def put(scr, rows):
    for f, v in enumerate(rows):
        scr[8 * f : 8 * f + 8, :] = v


def prepare_near(seg, nft, spread, scr):
    k = lax.broadcasted_iota(jnp.int32, (K, 384), 0) - KNUM
    a = lax.broadcasted_iota(jnp.int32, (K, 384), 1) // 128
    pick = (k == a) | (k == a + 6) | (k == a + 12)
    pick = jnp.where(pick, 1.0, 0.0).astype(bf16)

    def body(g, carry):
        tiles = pl.ds(pl.multiple_of(g * 8, 8), 8)
        comp = [seg[i, tiles, :] for i in range(9)]
        put(scr, near_rows(comp[0:3], comp[3:6], comp[6:9]))
        for c in range(8):
            feat = scr[pl.ds(c, K, stride=8), :]
            feat = jnp.concatenate([feat, jnp.zeros((128 - K, 128), f32)], 0).T.astype(bf16)
            nft[g * 8 + c] = feat
            wide = jnp.dot(feat[:, :K], pick, preferred_element_type=f32)
            for i in range(3):
                spread[g * 8 + c, 128 * i : 128 * i + 128, :] = wide[:, 128 * i : 128 * i + 128]
        return carry

    lax.fori_loop(0, 16, body, 0)
    lane = lax.broadcasted_iota(jnp.int32, (128, 128), 1)
    nft[128] = jnp.where(lane == KNUM + 18, 1.0, 0.0).astype(bf16)
    spread[128] = jnp.zeros((384, 128), f32)


def block(comp, nears, nft, spread, scr, part):
    x, b, l = comp[0:3], comp[3:6], comp[6:9]
    put(scr, far_rows(x, b, l))
    near_parts = []
    zn = jnp.zeros((KNUM, 128), bf16)
    zd = jnp.zeros((KDIST, 128), bf16)
    for c in range(8):
        feat = scr[pl.ds(c, K, stride=8), :].astype(bf16)
        xf = scr[pl.ds(8 * K + c, 16, stride=8), :].astype(bf16)
        right = jnp.concatenate(
            [
                jnp.concatenate([feat[:KNUM], zn], 1),
                jnp.concatenate([zd, feat[KNUM:]], 1),
            ],
            0,
        )
        n = nears[c]
        both = jnp.dot(nft[n][:, :K], right, preferred_element_type=f32)
        inv = lax.rsqrt(both[:, 128:])
        coup = both[:, :128] * (inv * inv * inv)
        hi = coup.astype(bf16)
        lo = (coup - hi.astype(f32)).astype(bf16)
        sn = lax.dot_general(
            jnp.concatenate([xf, xf], 1),
            jnp.concatenate([hi, lo], 1),
            NT,
            preferred_element_type=f32,
        )
        near_parts.append(sn[0:8] + sn[8:16])
        acc = [None] * 4
        for i in range(16):
            cv = coup[8 * i : 8 * i + 8]
            for a in range(3):
                t = cv * spread[n, 128 * a + 8 * i : 128 * a + 8 * i + 8, :]
                acc[a] = t if acc[a] is None else acc[a] + t
            acc[3] = cv if acc[3] is None else acc[3] + cv
        for a in range(4):
            part[64 * a + 8 * c : 64 * a + 8 * c + 8, :] = acc[a]
    sums = []
    for a in range(4):
        s = part[pl.ds(64 * a, 8, stride=8), :]
        for i in range(1, 8):
            s = s + part[pl.ds(64 * a + i, 8, stride=8), :]
        sums.append(s)
    far = [x[a] * sums[3] - sums[a] for a in range(3)]
    return far, near_parts


FIRST = 23


def shifted(d, s, j, sign):
    k = (j * 101) & 127
    dx, dz, dy, dc = k >> 5, (k >> 3) & 3, (k >> 1) & 3, k & 1
    if sign < 0:
        dx, dz, dy = 4 - dx, 4 - dz, 4 - dy
    x = ((d >> 2) + dx) & 3
    z = ((d & 3) + dz) & 3
    y = ((s >> 1) + dy) & 3
    c = ((s & 1) + dc) & 1
    return x * 4 + z, y * 2 + c


def exchange(
    seg_hbm, send_hbm, local_hbm, remote_hbm, count_hbm, cell_hbm,
    out_ref,
    send_smem, send_ref, local_ref, remote_ref, count_ref, cell_ref,
    seg, tiles, stage, recv, back, nraw, nft, spread, nscr, scr, part, mom, mom_a, mom_b, nrow, near_smem,
    seg_sem, out_send, out_recv, back_send, back_recv, mom_sem, row_sem, arg_sem, stage_sem,
):
    d = lax.axis_index("dom")
    s = lax.axis_index("sub")
    me = d * 8 + s
    barrier = pltpu.get_barrier_semaphore()
    for k in range(1, 8):
        pl.semaphore_signal(barrier, inc=1, device_id=(d, (s + k) & 7), device_id_type=MESH)
    for k in range(1, 16):
        pl.semaphore_signal(barrier, inc=1, device_id=((d + k) & 15, s), device_id_type=MESH)
    load = pltpu.make_async_copy(seg_hbm, seg, seg_sem)
    load.start()
    moves = [
        (send_hbm, send_smem), (local_hbm, local_ref), (remote_hbm, remote_ref),
        (count_hbm, count_ref), (cell_hbm, cell_ref), (send_hbm, send_ref),
    ]
    moves = [pltpu.make_async_copy(a, b, arg_sem.at[i]) for i, (a, b) in enumerate(moves)]
    for move in moves:
        move.start()
    load.wait()
    for g in range(16):
        for a in range(9):
            tiles[8 * g : 8 * g + 8, a, :] = seg[a, 8 * g : 8 * g + 8, :]
    for move in moves:
        move.wait()

    def gather(j):
        td, ts = shifted(d, s, j, 1)
        there = td * 8 + ts
        for c in range(CAP):
            stage[j, 9 * c : 9 * c + 9, :] = tiles[send_smem[c, there]]
        return td, ts

    def send(j, carry):
        partner = gather(j)
        pltpu.make_async_remote_copy(
            src_ref=stage.at[j], dst_ref=recv.at[pl.ds(pl.multiple_of(j * 40, 8), 36)],
            send_sem=out_send, recv_sem=out_recv.at[j // GROUP],
            device_id=partner, device_id_type=MESH).start()
        return carry

    pl.semaphore_wait(barrier, 22)
    for k in range(1, 8):
        pl.semaphore_signal(stage_sem, inc=1, device_id=(d, (s + k) & 7), device_id_type=MESH)
    pl.semaphore_wait(stage_sem, 7)
    lax.fori_loop(1, FIRST, send, 0)

    lane = lax.broadcasted_iota(jnp.int32, (128, 128), 1)
    cells = lax.broadcasted_iota(jnp.int32, (128, 128), 0)
    onehot = jnp.where(cells == cell_ref[...], 1.0, 0.0)
    outer = jnp.zeros((128, 128), f32)
    for a in range(3):
        for b in range(3):
            total = jnp.sum(seg[3 + a] * seg[6 + b], axis=1, keepdims=True)
            outer = jnp.where(lane == 3 * a + b, total, outer)
    sums = jnp.dot(onehot, outer, precision=EXACT, preferred_element_type=f32).T
    last = jnp.concatenate([jnp.zeros((1, NCELL), f32), sums[8:9, :NCELL]], 1)
    mom[...] = sums[0:8] + jnp.concatenate([last, jnp.zeros((7, 128), f32)], 0)
    mom_a[0] = mom[...]
    for k in range(1, 8):
        pltpu.make_async_remote_copy(
            src_ref=mom, dst_ref=mom_a.at[k], send_sem=mom_sem.at[0], recv_sem=mom_sem.at[1],
            device_id=(d, (s + k) & 7), device_id_type=MESH).start()

    lax.fori_loop(FIRST, PEERS, send, 0)
    gather(0)
    recv[0:36, :] = stage[0]

    remote = remote_ref[...]
    slot = (remote & 3) * 128 + (remote >> 2)
    pair = lax.broadcasted_iota(jnp.int32, (1, 512), 1)
    value = jnp.where(pair < count_ref[0], local_ref[...], 128).astype(f32).astype(bf16)
    value = jnp.broadcast_to(value, (16, 512))
    rows = lax.broadcasted_iota(jnp.int32, (128, 512), 0)
    for c in range(CAP):
        here = jnp.where(rows + 128 * c == slot, 1.0, 0.0).astype(bf16)
        row = lax.dot_general(value, here, NT, preferred_element_type=f32)
        nrow[c : c + 1, :] = jnp.clip(row[0:1].astype(jnp.int32), 0, 128)
    nrow[4:8, :] = jnp.zeros((4, 128), jnp.int32)
    to_smem = pltpu.make_async_copy(nrow, near_smem, row_sem)
    to_smem.start()
    prepare_near(seg, nft, spread, nscr)

    a_all = pltpu.make_async_remote_copy(
        src_ref=mom_a.at[pl.ds(1, 7)], dst_ref=mom_a.at[pl.ds(1, 7)], send_sem=mom_sem.at[0], recv_sem=mom_sem.at[1],
        device_id=(d, (s + 1) & 7), device_id_type=MESH)
    a_all.wait()
    mom_b[0] = jnp.sum(mom_a[...], 0)
    for k in range(1, 16):
        pltpu.make_async_remote_copy(
            src_ref=mom_b.at[0], dst_ref=mom_b.at[k], send_sem=mom_sem.at[2], recv_sem=mom_sem.at[3],
            device_id=((d + k) & 15, s), device_id_type=MESH).start()
    to_smem.wait()

    def wait_blocks(count, g):
        pltpu.make_async_remote_copy(
            src_ref=stage.at[pl.ds(0, count)], dst_ref=stage.at[pl.ds(0, count)],
            send_sem=out_send, recv_sem=out_recv.at[g],
            device_id=shifted(d, s, 1, 1), device_id_type=MESH).wait_recv()

    low = lax.broadcasted_iota(jnp.int32, (8, 128), 0) < CAP

    def work(g, carry):
        @pl.when(g == 0)
        def _():
            wait_blocks(GROUP - 1, 0)

        @pl.when(g > 0)
        def _():
            wait_blocks(GROUP, g)

        for u in range(GROUP // 2):
            j = g * GROUP + 2 * u
            first = pl.multiple_of(j * 40, 8)
            comp = []
            for a in range(9):
                even = recv[pl.ds(first + a, 8, stride=9), :]
                odd = recv[pl.ds(first + 4 + a, 8, stride=9), :]
                comp.append(jnp.where(low, even, odd))
            who = []
            for v in range(2):
                td, ts = shifted(d, s, j + v, -1)
                who.append(td * 8 + ts)
            nears = [jnp.clip(near_smem[c, who[v]], 0, 128) for v in range(2) for c in range(CAP)]
            far, near = block(comp, nears, nft, spread, scr.at[u], part.at[u])
            for v in range(2):
                for a in range(3):
                    recv[pl.ds(first + 40 * v + CAP * a, CAP), :] = far[a][CAP * v : CAP * v + CAP]
                for c in range(CAP):
                    nraw[pl.ds(pl.multiple_of(who[v] * 16, 16) + 4 * c, 4), :] = near[CAP * v + c][0:4]

        for u in range(GROUP):
            j = g * GROUP + u

            @pl.when(j > 0)
            def _():
                pltpu.make_async_remote_copy(
                    src_ref=recv.at[pl.ds(pl.multiple_of(j * 40, 8), 12)],
                    dst_ref=back.at[pl.ds(pl.multiple_of(me * 16, 16), 12)],
                    send_sem=back_send, recv_sem=back_recv,
                    device_id=shifted(d, s, j, -1), device_id_type=MESH).start()

        return carry

    lax.fori_loop(0, PEERS // GROUP, work, 0)
    back[pl.ds(pl.multiple_of(me * 16, 16), 12), :] = recv[0:12, :]

    b_all = pltpu.make_async_remote_copy(
        src_ref=mom_b.at[pl.ds(1, 15)], dst_ref=mom_b.at[pl.ds(1, 15)], send_sem=mom_sem.at[2], recv_sem=mom_sem.at[3],
        device_id=((d + 1) & 15, s), device_id_type=MESH)
    b_all.wait()
    packed = jnp.sum(mom_b[...], 0)
    sums = [packed[r : r + 1, :NCELL] for r in range(8)] + [packed[0:1, NCELL:]]
    scale = 0.5 / math.sqrt(PEERS * 128 * 128)
    sym = [(sums[3 * a + b] + sums[3 * b + a]) * scale for a in range(3) for b in range(3)]
    sym = jnp.concatenate(sym + [jnp.zeros((128 - 9, NCELL), f32)], 0)
    moments = jnp.concatenate([sym, jnp.zeros((128, 128 - NCELL), f32)], 1).T
    rows = lax.broadcasted_iota(jnp.int32, (128, 128), 0)
    lanes = lax.broadcasted_iota(jnp.int32, (128, 128), 1)
    weights = 8.0 / (8.0 + jnp.abs(rows - lanes).astype(f32))
    stress = jnp.dot(weights, moments, precision=EXACT, preferred_element_type=f32)
    onehot = jnp.where(rows == cell_ref[...], 1.0, 0.0).T
    ts = jnp.dot(onehot, stress, precision=EXACT, preferred_element_type=f32)

    pick = jnp.concatenate([jnp.where(rows == nrow[c : c + 1, :], 1.0, 0.0).astype(bf16) for c in range(CAP)], 1)

    def gathered(ref, a, which):
        v = jnp.concatenate([ref[pl.ds(4 * c + a if which else 4 * a + c, 128, stride=16), :] for c in range(CAP)], 0)
        hi = v.astype(bf16)
        lo = (v - hi.astype(f32)).astype(bf16)
        return jnp.concatenate([hi, lo], 1)

    near = []
    for a in range(4):
        both = jnp.dot(pick, gathered(nraw, a, True), preferred_element_type=f32)
        near.append(both[:, :128] + both[:, 128:])
    for g in range(16):
        r = slice(8 * g, 8 * g + 8)
        pull = []
        for k in range(3):
            parts = [jnp.broadcast_to(ts[r, 3 * k + m : 3 * k + m + 1], (8, 128)) * seg[3 + m, r, :] for m in range(3)]
            pull.append(parts[0] + parts[1] + parts[2])
        line = [seg[6 + m, r, :] for m in range(3)]
        for a in range(3):
            p, q = (a + 1) % 3, (a + 2) % 3
            field = pull[p] * line[q] - pull[q] * line[p]
            out_ref[a, r, :] = seg[a, r, :] * near[3][r] - near[a][r] + field

    pltpu.make_async_remote_copy(
        src_ref=stage.at[pl.ds(1, PEERS - 1)], dst_ref=stage.at[pl.ds(1, PEERS - 1)], send_sem=out_send,
        recv_sem=out_recv.at[0], device_id=shifted(d, s, 1, 1), device_id_type=MESH).wait_send()
    pltpu.make_async_remote_copy(
        src_ref=stage.at[pl.ds(1, PEERS - 1), pl.ds(0, 12)], dst_ref=stage.at[pl.ds(1, PEERS - 1), pl.ds(0, 12)],
        send_sem=back_send, recv_sem=back_recv, device_id=shifted(d, s, 1, 1), device_id_type=MESH).wait()

    pick = jnp.concatenate([jnp.where(rows == send_ref[c : c + 1, :], 1.0, 0.0).astype(bf16) for c in range(CAP)], 1)
    for a in range(3):
        both = jnp.dot(pick, gathered(back, a, False), preferred_element_type=f32)
        out_ref[a] += both[:, :128] + both[:, 128:]


def on_device(segments, send_tiles, pair_local, pair_remote, pair_count, tile_cell):
    vm = pl.BlockSpec(memory_space=pltpu.VMEM)
    dma = pltpu.SemaphoreType.DMA
    slots = send_tiles[0].T
    forces = pl.pallas_call(
        exchange,
        out_shape=jax.ShapeDtypeStruct((3, 128, 128), f32),
        in_specs=[pl.BlockSpec(memory_space=pl.ANY)] * 6,
        out_specs=vm,
        scratch_shapes=[
            pltpu.SMEM((CAP, 128), jnp.int32),
            pltpu.VMEM((CAP, 128), jnp.int32),
            pltpu.VMEM((1, 512), jnp.int32),
            pltpu.VMEM((1, 512), jnp.int32),
            pltpu.SMEM((1,), jnp.int32),
            pltpu.VMEM((1, 128), jnp.int32),
            pltpu.VMEM((9, 128, 128), f32),
            pltpu.VMEM((128, 9, 128), f32),
            pltpu.VMEM((PEERS, 36, 128), f32),
            pltpu.VMEM((PEERS * 40, 128), f32),
            pltpu.VMEM((PEERS * 16, 128), f32),
            pltpu.VMEM((PEERS * 16, 128), f32),
            pltpu.VMEM((129, 128, 128), bf16),
            pltpu.VMEM((129, 384, 128), f32),
            pltpu.VMEM((8 * K, 128), f32),
            pltpu.VMEM((GROUP // 2, 8 * FROWS, 128), f32),
            pltpu.VMEM((GROUP // 2, 256, 128), f32),
            pltpu.VMEM((8, 128), f32),
            pltpu.VMEM((8, 8, 128), f32),
            pltpu.VMEM((16, 8, 128), f32),
            pltpu.VMEM((8, 128), jnp.int32),
            pltpu.SMEM((8, 128), jnp.int32),
            dma(()),
            dma(()),
            dma((PEERS // GROUP,)),
            dma(()),
            dma(()),
            dma((4,)),
            dma(()),
            dma((6,)),
            pltpu.SemaphoreType.REGULAR,
        ],
        compiler_params=pltpu.CompilerParams(
            collective_id=0, has_side_effects=True, vmem_limit_bytes=58 << 20
        ),
    )(
        segments.transpose(1, 0, 2),
        slots,
        pair_local,
        pair_remote,
        pair_count,
        tile_cell.reshape(1, -1),
    )
    return forces.transpose(1, 0, 2)


def solution(mesh):
    in_specs = (
        P(("dom", "sub"), None, None),
        P(("dom", "sub"), None, None),
        P(("dom", "sub"), None),
        P(("dom", "sub"), None),
        P(("dom", "sub")),
        P(("dom", "sub")),
    )
    out_specs = P(("dom", "sub"), None, None)
    return jax.shard_map(
        on_device, mesh=mesh, in_specs=in_specs, out_specs=out_specs, check_vma=False
    )
```
